512 devices in a mesh: dp: 16 (over y, x_lo, core), mp: 32 (over z, x_hi).
Axes of the slice: x: 4 (x_hi: 2, x_lo: 2; x = x_hi * 2 + x_lo), y: 4, z: 16, core: 2. Of those that a mesh axis runs over, the one named last changes fastest.
Arguments:
- points: bfloat16 [16384, 1024], P('dp'), may hold values from -24 to 24
- fine_centroids: float32 [32768, 1024], P('mp', 'dp'), may hold values from -4 to 4
- coarse_centroids: float32 [4096, 1024], P('dp'), may hold values from -4 to 4
Outputs:
- new_fine: float32 [32768, 1024], P('mp', 'dp')
- new_coarse: float32 [4096, 1024], P('dp')
The draws below stay inside these ranges and needn't reach their ends.
All inputs are finite; a program needn't handle non-finite values.
Results may differ from the reference program's by a relative error of at most 0.01.
Values may be sent and summed in bfloat16 or wider, within the bound.
No kernel may reach another device: no remote copies, remote signals or barrier semaphores. Data moves between devices by JAX's collectives and lax.ppermute only.
A program may use at most 64 MiB of HBM per device.

```python
import math
import jax
import jax.numpy as jnp
from jax import lax

D = 1024
K1_DEV = 1024
NPTS = 16384
K1 = 32768
K2 = 4096


def shared_parts(key):
    centroids = jnp.clip(jax.random.normal(jax.random.fold_in(key, 101), (K1, D), jnp.float32), -4.0, 4.0)
    groups = K1 // K1_DEV
    aligned = min(8, K1_DEV // 4)
    targets = jnp.clip(jax.random.normal(jax.random.fold_in(key, 104), (groups, D), jnp.float32), -3.5, 3.5)
    jitter = jax.random.normal(jax.random.fold_in(key, 105), (groups, aligned, D), jnp.float32)
    shaped = centroids.reshape(groups, K1_DEV, D)
    shaped = shaped.at[:, :aligned, :].set(targets[:, None, :] + 0.3 * jitter)
    centroids = jnp.clip(shaped.reshape(K1, D), -4.0, 4.0)
    return (centroids, targets)


def draw_fine_centroids(key, part):
    centroids, targets = shared_parts(key)
    return centroids


def draw_points(key, part):
    key = jax.random.fold_in(key, 2)
    ramp = (0.5 * jnp.exp(math.log(4.0) * jnp.arange(NPTS, dtype=jnp.float32) / (NPTS - 1)))[:, None]
    values = jax.random.normal(jax.random.fold_in(key, 11), (NPTS, D), jnp.float32)
    spread = jnp.exp(jax.random.uniform(jax.random.fold_in(key, 12), (NPTS, 1), jnp.float32, 0.0, math.log(2.0)))
    result = values * ramp * spread
    return jnp.clip(result, -24.0, 24.0).astype(jnp.bfloat16)


def draw_coarse_centroids(key, part):
    centroids, targets = shared_parts(key)
    key = jax.random.fold_in(key, 3)
    groups = K1 // K1_DEV
    target_rows = jnp.arange(groups, dtype=jnp.int32) * (K2 // groups)
    values = jax.random.normal(jax.random.fold_in(key, 21), (K2, D), jnp.float32)
    values = values.at[target_rows].set(targets)
    return jnp.clip(values, -4.0, 4.0)


def setup_inputs(seed: int = 0) -> dict:
    key_of = jax.random.split(jax.random.key(seed), 4)
    return {
        "points": draw_points(jax.random.fold_in(key_of[3], 71), 0),
        "fine_centroids": draw_fine_centroids(jax.random.fold_in(key_of[3], 71), 0),
        "coarse_centroids": draw_coarse_centroids(jax.random.fold_in(key_of[3], 71), 0),
    }


PRIOR = 1.0

def assign(point_block, centroids_b, square_norms):
    products = jnp.dot(point_block, centroids_b.T, preferred_element_type=jnp.float32)
    scores = (2.0 * products - square_norms[None, :]) / math.sqrt(D)
    highest = lax.optimization_barrier(jnp.max(scores, axis=1, keepdims=True))
    weights = jnp.exp(scores - highest)
    return weights / lax.optimization_barrier(jnp.sum(weights, axis=1, keepdims=True))

def em_step(points, centroids):
    centroids_b = centroids.astype(jnp.bfloat16)
    square_norms = lax.optimization_barrier(jnp.sum(jnp.square(centroids_b.astype(jnp.float32)), axis=1))
    row_count = points.shape[0]
    block_rows = math.gcd(row_count, 512)
    blocks = points.astype(jnp.bfloat16).reshape(row_count // block_rows, block_rows, points.shape[1])

    def visit(running, point_block):
        numerator, counts = running
        assigned = assign(point_block, centroids_b, square_norms)
        numerator = numerator + jnp.dot(assigned.astype(jnp.bfloat16).T, point_block, preferred_element_type=jnp.float32)
        counts = counts + lax.optimization_barrier(jnp.sum(assigned, axis=0))
        return ((numerator, counts), None)
    start_state = (jnp.zeros(centroids.shape, jnp.float32), jnp.zeros((centroids.shape[0],), jnp.float32))
    (numerator, counts), _ = lax.scan(visit, start_state, blocks)
    return (numerator + centroids) / (counts + PRIOR)[:, None]

def reference(points, fine_centroids, coarse_centroids):
    new_fine = em_step(points, fine_centroids)
    new_coarse = em_step(new_fine, coarse_centroids)
    return (new_fine, new_coarse)
```

```python
import functools
import math

import jax
import jax.numpy as jnp
from jax import lax
from jax.experimental import pallas as pl
from jax.experimental.pallas import tpu as pltpu
from jax.sharding import Mesh, PartitionSpec as P

PRIOR = 1.0
F32, BF16 = jnp.float32, jnp.bfloat16
LANES = 128
PAIR = [(0, 1), (1, 0)]
CHIPS = ("y", "xl")
NEAR = ("zl", "xh")
CHIP_COUNT = 8
VMEM = pl.BlockSpec(memory_space=pltpu.VMEM)
SMEM = pl.BlockSpec(memory_space=pltpu.SMEM)
PARAMS = pltpu.CompilerParams(vmem_limit_bytes=24 * 1024 * 1024)


def shape_of(shape, dtype):
    return jax.ShapeDtypeStruct(shape, dtype)


def call(kernel, out_shape, scalars, arrays, scratch=(), cost=None):
    specs = [SMEM] * len(scalars) + [VMEM] * len(arrays)
    outs = jax.tree.map(lambda _: VMEM, out_shape)
    return pl.pallas_call(
        kernel, out_shape=out_shape, in_specs=specs, out_specs=outs,
        scratch_shapes=list(scratch), compiler_params=PARAMS, cost_estimate=cost,
    )(*scalars, *arrays)


def spread(block, axis, size):
    return exchange(jnp.broadcast_to(block[None], (size,) + block.shape), axis)


def exchange(blocks, axis):
    return lax.all_to_all(blocks, axis, split_axis=0, concat_axis=0, tiled=True)


def swap(block, axis):
    return lax.ppermute(block, axis, PAIR)


def to_row(column):
    return jnp.broadcast_to(column, (column.shape[0], LANES)).T[0:1, :]


def high_low(value):
    high = value.astype(BF16)
    return high, (value - high.astype(F32)).astype(BF16)


def flat(ref):
    return ref[...].reshape(ref.shape[0] * ref.shape[1], ref.shape[2])


def by_core(columns):
    groups, part = CHIP_COUNT, columns.shape[0] // (2 * CHIP_COUNT)
    columns = columns.reshape(groups, 2, part, columns.shape[1])
    return [columns[:, core].reshape(groups * part, columns.shape[3]) for core in range(2)]


def first_kernel(fine_ref, out_ref):
    out_ref[...] = jnp.broadcast_to(fine_ref[...].astype(BF16)[None], out_ref.shape)


def coarse_split_kernel(sizes, coarse_ref, coarse_c_ref, mine_ref, core_ref):
    core = lax.axis_index("c")
    slots = (core, 1 - core)
    own = mine_ref.shape[0]
    block = (lax.axis_index("zl") * sizes["xh"] + lax.axis_index("xh")) * sizes["zh"] + lax.axis_index("zh")
    mine_ref[...] = coarse_ref[pl.ds(pl.multiple_of(block * own, own), own), :]
    core_ref[...] = jnp.full(core_ref.shape, core, jnp.int32)
    for at, columns in enumerate(by_core(coarse_ref[...].astype(BF16).T)):
        coarse_c_ref[slots[at]] = columns.T


def own_scores_kernel(points_ref, own_ref, turned_ref, rest_ref, products_ref, norms_ref):
    core = lax.axis_index("c")
    slots = (core, 1 - core)
    own = flat(own_ref)
    norms_ref[...] = norms_of(own)
    n = products_ref.shape[0]
    tile = min(256, n)
    for start in range(0, n, tile):
        for at, columns in enumerate(by_core(points_ref[start:start + tile, :].T)):
            turned_ref[slots[at], :, start:start + tile] = columns
        rest_ref[start:start + tile, :] = turned_ref[1, :, start:start + tile].T
        products_ref[start:start + tile, :] = jnp.dot(
            turned_ref[0, :, start:start + tile].T, own, preferred_element_type=F32
        )


def norms_of(features):
    total = jnp.zeros((1, features.shape[1]), F32)
    for start in range(0, features.shape[0], LANES):
        total = total + jnp.sum(jnp.square(features[start:start + LANES].astype(F32)), axis=0, keepdims=True)
    return total


def fine_scores_kernel(scale, points_ref, products_ref, norms_ref, other_ref, w_ref, high_ref, lse_ref):
    other = flat(other_ref)
    norms = (norms_ref[...] + norms_of(other)) / scale
    n = products_ref.shape[0]
    tile = min(256, n)
    for start in range(0, n, tile):
        products = products_ref[start:start + tile, :] + jnp.dot(
            points_ref[start:start + tile, :], other, preferred_element_type=F32
        )
        scores = products * (2.0 / scale) - norms
        high = jnp.max(scores, axis=1, keepdims=True)
        weights = jnp.exp2(scores - high)
        w_ref[start:start + tile, :] = weights.astype(BF16)
        lse = to_row(high + jnp.log2(jnp.sum(weights, axis=1, keepdims=True)))
        high_ref[:, start:start + tile] = to_row(high)
        lse_ref[:, :, start:start + tile] = jnp.broadcast_to(lse[None], (lse_ref.shape[0], 1, tile))


def log_sum(ref):
    rows = ref[:, 0, :]
    top = jnp.max(rows, axis=0, keepdims=True)
    return top + jnp.log2(jnp.sum(jnp.exp2(rows - top), axis=0, keepdims=True))


def numer_send_kernel(points_t_ref, w_ref, high_ref, lses_ref, send_ref, factor_ref):
    factor = jnp.exp2(high_ref[...] - log_sum(lses_ref))
    factor_ref[...] = factor
    _, half, n = points_t_ref.shape
    scaled = (points_t_ref[1].astype(F32) * factor).astype(BF16)
    high, low = high_low(factor)
    left = jnp.concatenate([scaled, high, low, jnp.zeros((14, n), BF16)], axis=0)
    sums = jnp.dot(left, w_ref[...], preferred_element_type=F32)
    send_ref[0:half, :] = sums[0:half].astype(BF16)
    high, low = high_low(sums[half:half + 1] + sums[half + 1:half + 2])
    send_ref[half:half + 16, :] = jnp.concatenate([high, low, jnp.zeros((14, high.shape[1]), BF16)], axis=0)


def numer_keep_kernel(points_t_ref, w_ref, factor_ref, keep_ref):
    scaled = (points_t_ref[0].astype(F32) * factor_ref[...]).astype(BF16)
    keep_ref[...] = jnp.dot(scaled, w_ref[...], preferred_element_type=F32)


def pair_kernel(keep_ref, came_ref, sent_ref, out_ref):
    groups = out_ref.shape[0]
    half, k = keep_ref.shape
    part, blocks = half // groups, k // LANES
    numer = (keep_ref[...] + came_ref[0:half, :].astype(F32)).astype(BF16)
    tail = came_ref[half:half + 16, :].astype(F32) + sent_ref[half:half + 16, :].astype(F32)
    counts = tail[0:1] + tail[1:2]
    counts = jnp.concatenate([counts[:, at:at + LANES] for at in range(0, k, LANES)], axis=0)
    counts = jnp.concatenate(high_low(counts), axis=0)
    for group in range(groups):
        for block in range(blocks):
            out_ref[group, block * part:(block + 1) * part, :] = numer[
                group * part:(group + 1) * part, block * LANES:(block + 1) * LANES
            ]
        out_ref[group, blocks * part:blocks * part + 2 * blocks, :] = counts


def new_fine_kernel(came_ref, fine_ref, new_ref, send_ref):
    groups = came_ref.shape[0]
    part, k = new_ref.shape
    blocks = k // LANES
    counts = jnp.sum(came_ref[:, blocks * part:blocks * part + 2 * blocks, :].astype(F32), axis=0)
    counts = counts[0:blocks] + counts[blocks:2 * blocks] + PRIOR
    for block in range(blocks):
        lanes = slice(block * LANES, (block + 1) * LANES)
        numer = jnp.sum(came_ref[:, block * part:(block + 1) * part, :].astype(F32), axis=0)
        new = (numer + fine_ref[:, lanes]) / counts[block:block + 1]
        new_ref[:, lanes] = new
        send_ref[:, :, lanes] = jnp.broadcast_to(new.astype(BF16)[None], (groups, part, LANES))


def own_coarse_kernel(coarse_ref, own_ref, products_ref):
    products_ref[...] = jnp.dot(coarse_ref[0], flat(own_ref), preferred_element_type=F32)


def coarse_scores_kernel(scale, coarse_ref, products_ref, other_ref, w_ref, high_ref, lse_ref):
    norms = jnp.zeros((coarse_ref.shape[1], 1), F32)
    for half in range(2):
        norms = norms + jnp.sum(jnp.square(coarse_ref[half].astype(F32)), axis=1, keepdims=True)
    norms = norms / scale
    products = products_ref[...] + jnp.dot(coarse_ref[1], flat(other_ref), preferred_element_type=F32)
    scores = products * (2.0 / scale) - norms
    high = jnp.max(scores, axis=0, keepdims=True)
    weights = jnp.exp2(scores - high)
    w_ref[...] = weights
    high_ref[...] = high
    lse = high + jnp.log2(jnp.sum(weights, axis=0, keepdims=True))
    lse_ref[...] = jnp.broadcast_to(lse[None], lse_ref.shape)


def tail_of(counts):
    lane = lax.broadcasted_iota(jnp.int32, (counts.shape[0], LANES), 1)
    high = counts.astype(BF16).astype(F32)
    return jnp.where(lane == 0, high, jnp.where(lane == 1, counts - high, 0.0)).astype(BF16)


def coarse_numer_kernel(w_ref, high_ref, lses_ref, own_ref, other_ref, send_ref):
    factor = jnp.exp2(high_ref[...] - log_sum(lses_ref))
    blocks, rows, wide = send_ref.shape
    half_d = (wide - LANES) // 2
    assigned = w_ref[...] * factor
    assigned_b = assigned.astype(BF16)
    for at, ref in enumerate((own_ref, other_ref)):
        numer = lax.dot_general(
            assigned_b, flat(ref), (((1,), (1,)), ((), ())), preferred_element_type=F32
        )
        send_ref[:, :, at * half_d:(at + 1) * half_d] = numer.astype(BF16).reshape(blocks, rows, half_d)
    tail = tail_of(jnp.sum(assigned, axis=1, keepdims=True))
    send_ref[:, :, 2 * half_d:wide] = tail.reshape(blocks, rows, LANES)


def coarse_partial_kernel(came_ref, send_ref):
    far, own, wide = send_ref.shape
    d = wide - LANES
    sums = jnp.sum(came_ref[...].astype(F32), axis=0)
    send_ref[:, :, 0:d] = sums[:, 0:d].astype(BF16).reshape(far, own, d)
    tail = tail_of(sums[:, d:d + 1] + sums[:, d + 1:d + 2])
    send_ref[:, :, d:d + LANES] = tail.reshape(far, own, LANES)


def new_coarse_kernel(core_ref, came_ref, mine_ref, send_ref):
    d = send_ref.shape[2]
    half_d, part = d // 2, d // (2 * CHIP_COUNT)
    sums = jnp.sum(came_ref[...].astype(F32), axis=0)
    counts = sums[:, d:d + 1] + sums[:, d + 1:d + 2]
    first = core_ref[:, 0:1] == 0
    own, other = sums[:, 0:half_d], sums[:, half_d:d]
    by_core = (jnp.where(first, own, other), jnp.where(first, other, own))
    numer = jnp.concatenate(
        [by_core[core][:, at:at + part] for at in range(0, half_d, part) for core in range(2)], axis=1
    )
    new = (numer + mine_ref[...]) / (counts + PRIOR)
    send_ref[...] = jnp.broadcast_to(new.astype(BF16)[None], send_ref.shape)


def repeat_kernel(came_ref, send_ref):
    send_ref[...] = jnp.broadcast_to(flat(came_ref)[None], send_ref.shape)


def widen_kernel(came_ref, out_ref):
    out_ref[...] = flat(came_ref).astype(F32)


def local(sizes, points, fine_centroids, coarse_centroids):
    n, d = points.shape
    k, part = fine_centroids.shape
    rows = coarse_centroids.shape[0]
    groups, near, far = sizes["y"] * sizes["xl"], sizes["zl"] * sizes["xh"], sizes["zh"]
    scale = math.sqrt(d) * math.log(2.0)
    half_d, near_rows, own_rows = d // 2, rows // near, rows // (near * far)
    fine_t = fine_centroids.T

    coarse_c, mine, core = call(
        functools.partial(coarse_split_kernel, sizes),
        (shape_of((2, rows, half_d), BF16), shape_of((own_rows, d), F32), shape_of((own_rows, LANES), jnp.int32)),
        (), (coarse_centroids,),
    )
    own = exchange(call(first_kernel, shape_of((groups, part, k), BF16), (), (fine_t,)), CHIPS)
    other = swap(own, "c")
    turned, rest, products, norms = call(
        own_scores_kernel,
        (shape_of((2, half_d, n), BF16), shape_of((n, half_d), BF16), shape_of((n, k), F32), shape_of((1, k), F32)),
        (), (points, own),
        cost=pl.CostEstimate(flops=8 * n * d * k, bytes_accessed=48 * n * k, transcendentals=0),
    )
    w, high, lses = call(
        functools.partial(fine_scores_kernel, scale),
        (shape_of((n, k), BF16), shape_of((1, n), F32), shape_of((far * near, 1, n), F32)),
        (), (rest, products, norms, other),
    )
    lses = exchange(lses, ("zh",) + NEAR)
    send, factor = call(
        numer_send_kernel, (shape_of((half_d + 16, k), BF16), shape_of((1, n), F32)),
        (), (turned, w, high, lses),
    )
    came = swap(send, "c")
    keep = call(
        numer_keep_kernel, shape_of((half_d, k), F32), (), (turned, w, factor),
        cost=pl.CostEstimate(flops=n * d * k, bytes_accessed=6 * n * k, transcendentals=0),
    )
    tall = (part + 2) * (k // LANES)
    summed = exchange(call(pair_kernel, shape_of((groups, tall, LANES), BF16), (), (keep, came, send)), CHIPS)
    new_fine_t, blocks = call(
        new_fine_kernel, (shape_of((part, k), F32), shape_of((groups, part, k), BF16)), (), (summed, fine_t)
    )
    own = exchange(blocks, CHIPS)
    other = swap(own, "c")
    products = call(
        own_coarse_kernel, shape_of((rows, k), F32), (), (coarse_c, own),
        cost=pl.CostEstimate(flops=rows * d * k, bytes_accessed=6 * rows * k, transcendentals=0),
    )
    w, high, lses = call(
        functools.partial(coarse_scores_kernel, scale),
        (shape_of((rows, k), F32), shape_of((1, k), F32), shape_of((groups * 2, 1, k), F32)),
        (), (coarse_c, products, other),
    )
    lses = exchange(lses, CHIPS + ("c",))
    wide = d + LANES
    summed = call(coarse_numer_kernel, shape_of((near, near_rows, wide), BF16), (), (w, high, lses, own, other))
    summed = exchange(summed, NEAR)
    summed = exchange(call(coarse_partial_kernel, shape_of((far, own_rows, wide), BF16), (), (summed,)), "zh")
    blocks = call(new_coarse_kernel, shape_of((far, own_rows, d), BF16), (), (core, summed, mine))
    blocks = call(repeat_kernel, shape_of((near, near_rows, d), BF16), (), (exchange(blocks, "zh"),))
    new_coarse = call(widen_kernel, shape_of((rows, d), F32), (), (exchange(blocks, NEAR),))
    return (new_fine_t.T, new_coarse)


def solution(mesh):
    sizes = {"y": 4, "xl": 2, "c": 2, "zh": 8, "zl": 2, "xh": 2}
    fine_mesh = Mesh(mesh.devices.reshape(tuple(sizes.values())), tuple(sizes))
    dp, mp = ("y", "xl", "c"), ("zh", "zl", "xh")
    in_specs = (P(dp, None), P(mp, dp), P(dp, None))
    out_specs = (P(mp, dp), P(dp, None))
    run = functools.partial(local, sizes)
    return jax.shard_map(run, mesh=fine_mesh, in_specs=in_specs, out_specs=out_specs, check_vma=False)
```

```python
import functools
import math

import jax
import jax.numpy as jnp
from jax import lax
from jax.experimental import pallas as pl
from jax.experimental.pallas import tpu as pltpu
from jax.sharding import Mesh, PartitionSpec as P

PRIOR = 1.0
F32, BF16 = jnp.float32, jnp.bfloat16
LANES = 128
PAIR = [(0, 1), (1, 0)]
CHIPS = ("xl", "y")
NEAR = ("xh", "zl")
CHIP_COUNT = 8
ORDER = (0, 2, 4, 6, 1, 3, 5, 7)
ORDER_BACK = (0, 4, 1, 5, 2, 6, 3, 7)
VMEM = pl.BlockSpec(memory_space=pltpu.VMEM)
SMEM = pl.BlockSpec(memory_space=pltpu.SMEM)
PARAMS = pltpu.CompilerParams(vmem_limit_bytes=24 * 1024 * 1024)


def shape_of(shape, dtype):
    return jax.ShapeDtypeStruct(shape, dtype)


def call(kernel, out_shape, scalars, arrays, scratch=(), cost=None):
    specs = [SMEM] * len(scalars) + [VMEM] * len(arrays)
    outs = jax.tree.map(lambda _: VMEM, out_shape)
    return pl.pallas_call(
        kernel, out_shape=out_shape, in_specs=specs, out_specs=outs,
        scratch_shapes=list(scratch), compiler_params=PARAMS, cost_estimate=cost,
    )(*scalars, *arrays)


def spread(block, axis, size):
    return exchange(jnp.broadcast_to(block[None], (size,) + block.shape), axis)


def exchange(blocks, axis):
    return lax.all_to_all(blocks, axis, split_axis=0, concat_axis=0, tiled=True)


def swap(block, axis):
    return lax.ppermute(block, axis, PAIR)


def to_row(column):
    return jnp.broadcast_to(column, (column.shape[0], LANES)).T[0:1, :]


def high_low(value):
    high = value.astype(BF16)
    return high, (value - high.astype(F32)).astype(BF16)


def flat(ref):
    return ref[...].reshape(ref.shape[0] * ref.shape[1], ref.shape[2])


def by_core(columns):
    part = columns.shape[0] // (2 * CHIP_COUNT)
    parts = [columns[at:at + part] for at in range(0, columns.shape[0], part)]
    return [jnp.concatenate([parts[2 * chip + core] for chip in ORDER], axis=0) for core in range(2)]


def first_kernel(fine_ref, out_ref):
    out_ref[...] = jnp.broadcast_to(fine_ref[...].astype(BF16)[None], out_ref.shape)


def coarse_split_kernel(sizes, coarse_ref, coarse_c_ref, mine_ref, core_ref):
    core = lax.axis_index("c")
    slots = (core, 1 - core)
    own = mine_ref.shape[0]
    block = (lax.axis_index("xh") * sizes["zl"] + lax.axis_index("zl")) * sizes["zh"] + lax.axis_index("zh")
    mine_ref[...] = coarse_ref[pl.ds(pl.multiple_of(block * own, own), own), :]
    core_ref[...] = jnp.full(core_ref.shape, core, jnp.int32)
    for at, columns in enumerate(by_core(coarse_ref[...].astype(BF16).T)):
        coarse_c_ref[slots[at]] = columns.T


def own_scores_kernel(points_ref, own_ref, turned_ref, rest_ref, products_ref, norms_ref):
    core = lax.axis_index("c")
    slots = (core, 1 - core)
    own = flat(own_ref)
    norms_ref[...] = norms_of(own)
    n = products_ref.shape[0]
    tile = min(256, n)
    for start in range(0, n, tile):
        for at, columns in enumerate(by_core(points_ref[start:start + tile, :].T)):
            turned_ref[slots[at], :, start:start + tile] = columns
        rest_ref[start:start + tile, :] = turned_ref[1, :, start:start + tile].T
        products_ref[start:start + tile, :] = jnp.dot(
            turned_ref[0, :, start:start + tile].T, own, preferred_element_type=F32
        )


def norms_of(features):
    total = jnp.zeros((1, features.shape[1]), F32)
    for start in range(0, features.shape[0], LANES):
        total = total + jnp.sum(jnp.square(features[start:start + LANES].astype(F32)), axis=0, keepdims=True)
    return total


def fine_scores_kernel(scale, points_ref, products_ref, norms_ref, other_ref, w_ref, high_ref, lse_ref):
    other = flat(other_ref)
    norms = (norms_ref[...] + norms_of(other)) / scale
    n = products_ref.shape[0]
    tile = min(256, n)
    for start in range(0, n, tile):
        products = products_ref[start:start + tile, :] + jnp.dot(
            points_ref[start:start + tile, :], other, preferred_element_type=F32
        )
        scores = products * (2.0 / scale) - norms
        high = jnp.max(scores, axis=1, keepdims=True)
        weights = jnp.exp2(scores - high)
        w_ref[start:start + tile, :] = weights.astype(BF16)
        lse = to_row(high + jnp.log2(jnp.sum(weights, axis=1, keepdims=True)))
        high_ref[:, start:start + tile] = to_row(high)
        lse_ref[:, :, start:start + tile] = jnp.broadcast_to(lse[None], (lse_ref.shape[0], 1, tile))


def log_sum(ref):
    rows = ref[:, 0, :]
    top = jnp.max(rows, axis=0, keepdims=True)
    return top + jnp.log2(jnp.sum(jnp.exp2(rows - top), axis=0, keepdims=True))


def numer_send_kernel(points_t_ref, w_ref, high_ref, lses_ref, send_ref, factor_ref):
    factor = jnp.exp2(high_ref[...] - log_sum(lses_ref))
    factor_ref[...] = factor
    _, half, n = points_t_ref.shape
    scaled = (points_t_ref[1].astype(F32) * factor).astype(BF16)
    high, low = high_low(factor)
    left = jnp.concatenate([scaled, high, low, jnp.zeros((14, n), BF16)], axis=0)
    sums = jnp.dot(left, w_ref[...], preferred_element_type=F32)
    send_ref[0:half, :] = sums[0:half].astype(BF16)
    high, low = high_low(sums[half:half + 1] + sums[half + 1:half + 2])
    send_ref[half:half + 16, :] = jnp.concatenate([high, low, jnp.zeros((14, high.shape[1]), BF16)], axis=0)


def numer_keep_kernel(points_t_ref, w_ref, factor_ref, keep_ref):
    scaled = (points_t_ref[0].astype(F32) * factor_ref[...]).astype(BF16)
    keep_ref[...] = jnp.dot(scaled, w_ref[...], preferred_element_type=F32)


def pair_kernel(keep_ref, came_ref, sent_ref, out_ref):
    groups = out_ref.shape[0]
    half, k = keep_ref.shape
    part, blocks = half // groups, k // LANES
    numer = (keep_ref[...] + came_ref[0:half, :].astype(F32)).astype(BF16)
    tail = came_ref[half:half + 16, :].astype(F32) + sent_ref[half:half + 16, :].astype(F32)
    counts = tail[0:1] + tail[1:2]
    counts = jnp.concatenate([counts[:, at:at + LANES] for at in range(0, k, LANES)], axis=0)
    counts = jnp.concatenate(high_low(counts), axis=0)
    for group in range(groups):
        for block in range(blocks):
            out_ref[group, block * part:(block + 1) * part, :] = numer[
                group * part:(group + 1) * part, block * LANES:(block + 1) * LANES
            ]
        out_ref[group, blocks * part:blocks * part + 2 * blocks, :] = counts


def new_fine_kernel(came_ref, fine_ref, new_ref, send_ref):
    groups = came_ref.shape[0]
    part, k = new_ref.shape
    blocks = k // LANES
    counts = jnp.sum(came_ref[:, blocks * part:blocks * part + 2 * blocks, :].astype(F32), axis=0)
    counts = counts[0:blocks] + counts[blocks:2 * blocks] + PRIOR
    for block in range(blocks):
        lanes = slice(block * LANES, (block + 1) * LANES)
        numer = jnp.sum(came_ref[:, block * part:(block + 1) * part, :].astype(F32), axis=0)
        new = (numer + fine_ref[:, lanes]) / counts[block:block + 1]
        new_ref[:, lanes] = new
        send_ref[:, :, lanes] = jnp.broadcast_to(new.astype(BF16)[None], (groups, part, LANES))


def own_coarse_kernel(coarse_ref, own_ref, products_ref):
    products_ref[...] = jnp.dot(coarse_ref[0], flat(own_ref), preferred_element_type=F32)


def coarse_scores_kernel(scale, coarse_ref, products_ref, other_ref, w_ref, high_ref, lse_ref):
    norms = jnp.zeros((coarse_ref.shape[1], 1), F32)
    for half in range(2):
        norms = norms + jnp.sum(jnp.square(coarse_ref[half].astype(F32)), axis=1, keepdims=True)
    norms = norms / scale
    products = products_ref[...] + jnp.dot(coarse_ref[1], flat(other_ref), preferred_element_type=F32)
    scores = products * (2.0 / scale) - norms
    high = jnp.max(scores, axis=0, keepdims=True)
    weights = jnp.exp2(scores - high)
    w_ref[...] = weights
    high_ref[...] = high
    lse = high + jnp.log2(jnp.sum(weights, axis=0, keepdims=True))
    lse_ref[...] = jnp.broadcast_to(lse[None], lse_ref.shape)


def tail_of(counts):
    lane = lax.broadcasted_iota(jnp.int32, (counts.shape[0], LANES), 1)
    high = counts.astype(BF16).astype(F32)
    return jnp.where(lane == 0, high, jnp.where(lane == 1, counts - high, 0.0)).astype(BF16)


def coarse_numer_kernel(w_ref, high_ref, lses_ref, own_ref, other_ref, send_ref):
    factor = jnp.exp2(high_ref[...] - log_sum(lses_ref))
    blocks, rows, wide = send_ref.shape
    half_d = (wide - LANES) // 2
    assigned = w_ref[...] * factor
    assigned_b = assigned.astype(BF16)
    for at, ref in enumerate((own_ref, other_ref)):
        numer = lax.dot_general(
            assigned_b, flat(ref), (((1,), (1,)), ((), ())), preferred_element_type=F32
        )
        send_ref[:, :, at * half_d:(at + 1) * half_d] = numer.astype(BF16).reshape(blocks, rows, half_d)
    tail = tail_of(jnp.sum(assigned, axis=1, keepdims=True))
    send_ref[:, :, 2 * half_d:wide] = tail.reshape(blocks, rows, LANES)


def coarse_partial_kernel(came_ref, send_ref):
    far, own, wide = send_ref.shape
    d = wide - LANES
    sums = jnp.sum(came_ref[...].astype(F32), axis=0)
    send_ref[:, :, 0:d] = sums[:, 0:d].astype(BF16).reshape(far, own, d)
    tail = tail_of(sums[:, d:d + 1] + sums[:, d + 1:d + 2])
    send_ref[:, :, d:d + LANES] = tail.reshape(far, own, LANES)


def new_coarse_kernel(core_ref, came_ref, mine_ref, send_ref):
    d = send_ref.shape[2]
    half_d, part = d // 2, d // (2 * CHIP_COUNT)
    sums = jnp.sum(came_ref[...].astype(F32), axis=0)
    counts = sums[:, d:d + 1] + sums[:, d + 1:d + 2]
    first = core_ref[:, 0:1] == 0
    own, other = sums[:, 0:half_d], sums[:, half_d:d]
    by_core = (jnp.where(first, own, other), jnp.where(first, other, own))
    numer = jnp.concatenate(
        [by_core[core][:, at * part:(at + 1) * part] for at in ORDER_BACK for core in range(2)], axis=1
    )
    new = (numer + mine_ref[...]) / (counts + PRIOR)
    send_ref[...] = jnp.broadcast_to(new.astype(BF16)[None], send_ref.shape)


def repeat_kernel(came_ref, send_ref):
    send_ref[...] = jnp.broadcast_to(flat(came_ref)[None], send_ref.shape)


def widen_kernel(came_ref, out_ref):
    out_ref[...] = flat(came_ref).astype(F32)


def local(sizes, points, fine_centroids, coarse_centroids):
    n, d = points.shape
    k, part = fine_centroids.shape
    rows = coarse_centroids.shape[0]
    groups, near, far = sizes["y"] * sizes["xl"], sizes["zl"] * sizes["xh"], sizes["zh"]
    scale = math.sqrt(d) * math.log(2.0)
    half_d, near_rows, own_rows = d // 2, rows // near, rows // (near * far)
    fine_t = fine_centroids.T

    coarse_c, mine, core = call(
        functools.partial(coarse_split_kernel, sizes),
        (shape_of((2, rows, half_d), BF16), shape_of((own_rows, d), F32), shape_of((own_rows, LANES), jnp.int32)),
        (), (coarse_centroids,),
    )
    own = exchange(call(first_kernel, shape_of((groups, part, k), BF16), (), (fine_t,)), CHIPS)
    other = swap(own, "c")
    turned, rest, products, norms = call(
        own_scores_kernel,
        (shape_of((2, half_d, n), BF16), shape_of((n, half_d), BF16), shape_of((n, k), F32), shape_of((1, k), F32)),
        (), (points, own),
        cost=pl.CostEstimate(flops=8 * n * d * k, bytes_accessed=48 * n * k, transcendentals=0),
    )
    w, high, lses = call(
        functools.partial(fine_scores_kernel, scale),
        (shape_of((n, k), BF16), shape_of((1, n), F32), shape_of((far * near, 1, n), F32)),
        (), (rest, products, norms, other),
    )
    lses = exchange(lses, NEAR + ("zh",))
    send, factor = call(
        numer_send_kernel, (shape_of((half_d + 16, k), BF16), shape_of((1, n), F32)),
        (), (turned, w, high, lses),
    )
    came = swap(send, "c")
    keep = call(
        numer_keep_kernel, shape_of((half_d, k), F32), (), (turned, w, factor),
        cost=pl.CostEstimate(flops=n * d * k, bytes_accessed=6 * n * k, transcendentals=0),
    )
    tall = (part + 2) * (k // LANES)
    summed = exchange(call(pair_kernel, shape_of((groups, tall, LANES), BF16), (), (keep, came, send)), CHIPS)
    new_fine_t, blocks = call(
        new_fine_kernel, (shape_of((part, k), F32), shape_of((groups, part, k), BF16)), (), (summed, fine_t)
    )
    own = exchange(blocks, CHIPS)
    other = swap(own, "c")
    products = call(
        own_coarse_kernel, shape_of((rows, k), F32), (), (coarse_c, own),
        cost=pl.CostEstimate(flops=rows * d * k, bytes_accessed=6 * rows * k, transcendentals=0),
    )
    w, high, lses = call(
        functools.partial(coarse_scores_kernel, scale),
        (shape_of((rows, k), F32), shape_of((1, k), F32), shape_of((groups * 2, 1, k), F32)),
        (), (coarse_c, products, other),
    )
    lses = exchange(lses, ("c",) + CHIPS)
    wide = d + LANES
    summed = call(coarse_numer_kernel, shape_of((near, near_rows, wide), BF16), (), (w, high, lses, own, other))
    summed = exchange(summed, NEAR)
    summed = exchange(call(coarse_partial_kernel, shape_of((far, own_rows, wide), BF16), (), (summed,)), "zh")
    blocks = call(new_coarse_kernel, shape_of((far, own_rows, d), BF16), (), (core, summed, mine))
    blocks = call(repeat_kernel, shape_of((near, near_rows, d), BF16), (), (exchange(blocks, "zh"),))
    new_coarse = call(widen_kernel, shape_of((rows, d), F32), (), (exchange(blocks, NEAR),))
    return (new_fine_t.T, new_coarse)


def solution(mesh):
    sizes = {"y": 4, "xl": 2, "c": 2, "zh": 8, "zl": 2, "xh": 2}
    fine_mesh = Mesh(mesh.devices.reshape(tuple(sizes.values())), tuple(sizes))
    dp, mp = ("y", "xl", "c"), ("zh", "zl", "xh")
    in_specs = (P(dp, None), P(mp, dp), P(dp, None))
    out_specs = (P(mp, dp), P(dp, None))
    run = functools.partial(local, sizes)
    return jax.shard_map(run, mesh=fine_mesh, in_specs=in_specs, out_specs=out_specs, check_vma=False)
```

```python
import functools
import math

import jax
import jax.numpy as jnp
from jax import lax
from jax.experimental import pallas as pl
from jax.experimental.pallas import tpu as pltpu
from jax.sharding import Mesh, PartitionSpec as P

PRIOR = 1.0
F32, BF16 = jnp.float32, jnp.bfloat16
LANES = 128
PAIR = [(0, 1), (1, 0)]
CHIPS = ("xl", "y")
NEAR = ("xh", "zl")
CHIP_COUNT = 8
ORDER = (0, 2, 4, 6, 1, 3, 5, 7)
ORDER_BACK = (0, 4, 1, 5, 2, 6, 3, 7)
VMEM = pl.BlockSpec(memory_space=pltpu.VMEM)
SMEM = pl.BlockSpec(memory_space=pltpu.SMEM)
PARAMS = pltpu.CompilerParams(vmem_limit_bytes=24 * 1024 * 1024)


def shape_of(shape, dtype):
    return jax.ShapeDtypeStruct(shape, dtype)


def call(kernel, out_shape, scalars, arrays, scratch=(), cost=None):
    specs = [SMEM] * len(scalars) + [VMEM] * len(arrays)
    outs = jax.tree.map(lambda _: VMEM, out_shape)
    return pl.pallas_call(
        kernel, out_shape=out_shape, in_specs=specs, out_specs=outs,
        scratch_shapes=list(scratch), compiler_params=PARAMS, cost_estimate=cost,
    )(*scalars, *arrays)


def spread(block, axis, size):
    return exchange(jnp.broadcast_to(block[None], (size,) + block.shape), axis)


def exchange(blocks, axis):
    return lax.all_to_all(blocks, axis, split_axis=0, concat_axis=0, tiled=True)


def swap(block, axis):
    return lax.ppermute(block, axis, PAIR)


def to_row(column):
    return jnp.broadcast_to(column, (column.shape[0], LANES)).T[0:1, :]


def high_low(value):
    high = value.astype(BF16)
    return high, (value - high.astype(F32)).astype(BF16)


def flat(ref):
    return ref[...].reshape(ref.shape[0] * ref.shape[1], ref.shape[2])


def by_core(columns):
    part = columns.shape[0] // (2 * CHIP_COUNT)
    parts = [columns[at:at + part] for at in range(0, columns.shape[0], part)]
    return [jnp.concatenate([parts[2 * chip + core] for chip in ORDER], axis=0) for core in range(2)]


def first_kernel(fine_ref, out_ref):
    out_ref[...] = jnp.broadcast_to(fine_ref[...].astype(BF16)[None], out_ref.shape)


def coarse_split_kernel(sizes, coarse_ref, new_ref, coarse_c_ref, mine_ref, core_ref, new_fine_ref):
    core = lax.axis_index("c")
    slots = (core, 1 - core)
    own = mine_ref.shape[0]
    block = (lax.axis_index("xh") * sizes["zl"] + lax.axis_index("zl")) * sizes["zh"] + lax.axis_index("zh")
    mine_ref[...] = coarse_ref[pl.ds(pl.multiple_of(block * own, own), own), :]
    core_ref[...] = jnp.full(core_ref.shape, core, jnp.int32)
    new_fine_ref[...] = new_ref[...]
    for at, columns in enumerate(by_core(coarse_ref[...].astype(BF16).T)):
        coarse_c_ref[slots[at]] = columns.T


def own_scores_kernel(points_ref, own_ref, turned_ref, rest_ref, products_ref, norms_ref):
    core = lax.axis_index("c")
    slots = (core, 1 - core)
    own = flat(own_ref)
    norms_ref[...] = norms_of(own)
    n = products_ref.shape[0]
    tile = min(256, n)
    for start in range(0, n, tile):
        for at, columns in enumerate(by_core(points_ref[start:start + tile, :].T)):
            turned_ref[slots[at], :, start:start + tile] = columns
        rest_ref[start:start + tile, :] = turned_ref[1, :, start:start + tile].T
        products_ref[start:start + tile, :] = jnp.dot(
            turned_ref[0, :, start:start + tile].T, own, preferred_element_type=F32
        )


def norms_of(features):
    total = jnp.zeros((1, features.shape[1]), F32)
    for start in range(0, features.shape[0], LANES):
        total = total + jnp.sum(jnp.square(features[start:start + LANES].astype(F32)), axis=0, keepdims=True)
    return total


def fine_scores_kernel(scale, points_ref, products_ref, norms_ref, other_ref, w_ref, high_ref, lse_ref):
    other = flat(other_ref)
    norms = (norms_ref[...] + norms_of(other)) / scale
    n = products_ref.shape[0]
    tile = min(256, n)
    for start in range(0, n, tile):
        products = products_ref[start:start + tile, :] + jnp.dot(
            points_ref[start:start + tile, :], other, preferred_element_type=F32
        )
        scores = products * (2.0 / scale) - norms
        high = jnp.max(scores, axis=1, keepdims=True)
        weights = jnp.exp2(scores - high)
        w_ref[start:start + tile, :] = weights.astype(BF16)
        lse = to_row(high + jnp.log2(jnp.sum(weights, axis=1, keepdims=True)))
        high_ref[:, start:start + tile] = to_row(high)
        lse_ref[:, :, start:start + tile] = jnp.broadcast_to(lse[None], (lse_ref.shape[0], 1, tile))


def log_sum(ref):
    rows = ref[:, 0, :]
    top = jnp.max(rows, axis=0, keepdims=True)
    return top + jnp.log2(jnp.sum(jnp.exp2(rows - top), axis=0, keepdims=True))


def numer_send_kernel(points_t_ref, w_ref, high_ref, lses_ref, send_ref, factor_ref):
    factor = jnp.exp2(high_ref[...] - log_sum(lses_ref))
    factor_ref[...] = factor
    _, half, n = points_t_ref.shape
    scaled = (points_t_ref[1].astype(F32) * factor).astype(BF16)
    high, low = high_low(factor)
    left = jnp.concatenate([scaled, high, low, jnp.zeros((14, n), BF16)], axis=0)
    sums = jnp.dot(left, w_ref[...], preferred_element_type=F32)
    send_ref[0:half, :] = sums[0:half].astype(BF16)
    high, low = high_low(sums[half:half + 1] + sums[half + 1:half + 2])
    send_ref[half:half + 16, :] = jnp.concatenate([high, low, jnp.zeros((14, high.shape[1]), BF16)], axis=0)


def numer_keep_kernel(points_t_ref, w_ref, factor_ref, keep_ref):
    scaled = (points_t_ref[0].astype(F32) * factor_ref[...]).astype(BF16)
    keep_ref[...] = jnp.dot(scaled, w_ref[...], preferred_element_type=F32)


def pair_kernel(keep_ref, came_ref, sent_ref, out_ref):
    groups = out_ref.shape[0]
    half, k = keep_ref.shape
    part, blocks = half // groups, k // LANES
    numer = (keep_ref[...] + came_ref[0:half, :].astype(F32)).astype(BF16)
    tail = came_ref[half:half + 16, :].astype(F32) + sent_ref[half:half + 16, :].astype(F32)
    counts = tail[0:1] + tail[1:2]
    counts = jnp.concatenate([counts[:, at:at + LANES] for at in range(0, k, LANES)], axis=0)
    counts = jnp.concatenate(high_low(counts), axis=0)
    for group in range(groups):
        for block in range(blocks):
            out_ref[group, block * part:(block + 1) * part, :] = numer[
                group * part:(group + 1) * part, block * LANES:(block + 1) * LANES
            ]
        out_ref[group, blocks * part:blocks * part + 2 * blocks, :] = counts


def new_fine_kernel(came_ref, fine_ref, new_ref, send_ref):
    groups = came_ref.shape[0]
    part, k = new_ref.shape
    blocks = k // LANES
    counts = jnp.sum(came_ref[:, blocks * part:blocks * part + 2 * blocks, :].astype(F32), axis=0)
    counts = counts[0:blocks] + counts[blocks:2 * blocks] + PRIOR
    for block in range(blocks):
        lanes = slice(block * LANES, (block + 1) * LANES)
        numer = jnp.sum(came_ref[:, block * part:(block + 1) * part, :].astype(F32), axis=0)
        new = (numer + fine_ref[:, lanes]) / counts[block:block + 1]
        new_ref[:, lanes] = new
        send_ref[:, :, lanes] = jnp.broadcast_to(new.astype(BF16)[None], (groups, part, LANES))


def own_coarse_kernel(coarse_ref, own_ref, products_ref):
    products_ref[...] = jnp.dot(coarse_ref[0], flat(own_ref), preferred_element_type=F32)


def coarse_scores_kernel(scale, coarse_ref, products_ref, other_ref, w_ref, high_ref, lse_ref):
    norms = jnp.zeros((coarse_ref.shape[1], 1), F32)
    for half in range(2):
        norms = norms + jnp.sum(jnp.square(coarse_ref[half].astype(F32)), axis=1, keepdims=True)
    norms = norms / scale
    products = products_ref[...] + jnp.dot(coarse_ref[1], flat(other_ref), preferred_element_type=F32)
    scores = products * (2.0 / scale) - norms
    high = jnp.max(scores, axis=0, keepdims=True)
    weights = jnp.exp2(scores - high)
    w_ref[...] = weights
    high_ref[...] = high
    lse = high + jnp.log2(jnp.sum(weights, axis=0, keepdims=True))
    lse_ref[...] = jnp.broadcast_to(lse[None], lse_ref.shape)


def tail_of(counts):
    lane = lax.broadcasted_iota(jnp.int32, (counts.shape[0], LANES), 1)
    high = counts.astype(BF16).astype(F32)
    return jnp.where(lane == 0, high, jnp.where(lane == 1, counts - high, 0.0)).astype(BF16)


def coarse_numer_kernel(w_ref, high_ref, lses_ref, own_ref, other_ref, send_ref):
    factor = jnp.exp2(high_ref[...] - log_sum(lses_ref))
    assigned = w_ref[...] * factor
    assigned_b = assigned.astype(BF16)
    near, tall, _ = send_ref.shape
    rows = assigned.shape[0] // near
    lane_blocks = (tall - 16) // rows
    for half, ref in enumerate((own_ref, other_ref)):
        numer = lax.dot_general(
            assigned_b, flat(ref), (((1,), (1,)), ((), ())), preferred_element_type=F32
        ).astype(BF16).reshape(near, rows, lane_blocks // 2 * LANES)
        for block in range(lane_blocks // 2):
            at = (half * (lane_blocks // 2) + block) * rows
            send_ref[:, at:at + rows, :] = numer[:, :, block * LANES:(block + 1) * LANES]
    counts = to_row(jnp.sum(assigned, axis=1, keepdims=True))
    counts = jnp.concatenate([counts[:, at:at + LANES] for at in range(0, counts.shape[1], LANES)], axis=0)
    high = counts.astype(BF16).astype(F32)
    pad = jnp.zeros((16 - 2 * counts.shape[0], LANES), F32)
    tail = jnp.concatenate([high, counts - high, pad], axis=0).astype(BF16)
    send_ref[:, tall - 16:tall, :] = jnp.broadcast_to(tail[None], (near, 16, LANES))


def coarse_partial_kernel(came_ref, send_ref):
    far, own, wide = send_ref.shape
    rows, lane_blocks = far * own, wide // LANES - 1
    for block in range(lane_blocks):
        numer = jnp.sum(came_ref[:, block * rows:(block + 1) * rows, :].astype(F32), axis=0)
        send_ref[:, :, block * LANES:(block + 1) * LANES] = numer.astype(BF16).reshape(far, own, LANES)
    tail = jnp.sum(came_ref[:, lane_blocks * rows:lane_blocks * rows + 16, :].astype(F32), axis=0)
    counts = jnp.where(lax.axis_index("xh") == 0, tail[0:1] + tail[2:3], tail[1:2] + tail[3:4])
    column = jnp.broadcast_to(counts, (LANES, LANES)).T
    column = jnp.where(lax.axis_index("zl") == 0, column[0:rows], column[rows:2 * rows])
    send_ref[:, :, lane_blocks * LANES:wide] = tail_of(column[:, 0:1]).reshape(far, own, LANES)


def new_coarse_kernel(core_ref, came_ref, mine_ref, send_ref):
    d = send_ref.shape[2]
    half_d, part = d // 2, d // (2 * CHIP_COUNT)
    sums = jnp.sum(came_ref[...].astype(F32), axis=0)
    counts = sums[:, d:d + 1] + sums[:, d + 1:d + 2]
    first = core_ref[:, 0:1] == 0
    own, other = sums[:, 0:half_d], sums[:, half_d:d]
    by_core = (jnp.where(first, own, other), jnp.where(first, other, own))
    numer = jnp.concatenate(
        [by_core[core][:, at * part:(at + 1) * part] for at in ORDER_BACK for core in range(2)], axis=1
    )
    new = (numer + mine_ref[...]) / (counts + PRIOR)
    send_ref[...] = jnp.broadcast_to(new.astype(BF16)[None], send_ref.shape)


def repeat_kernel(came_ref, send_ref):
    send_ref[...] = jnp.broadcast_to(flat(came_ref)[None], send_ref.shape)


def widen_kernel(came_ref, out_ref):
    out_ref[...] = flat(came_ref).astype(F32)


def local(sizes, points, fine_centroids, coarse_centroids):
    n, d = points.shape
    k, part = fine_centroids.shape
    rows = coarse_centroids.shape[0]
    groups, near, far = sizes["y"] * sizes["xl"], sizes["zl"] * sizes["xh"], sizes["zh"]
    scale = math.sqrt(d) * math.log(2.0)
    half_d, near_rows, own_rows = d // 2, rows // near, rows // (near * far)
    fine_t = fine_centroids.T

    own = exchange(call(first_kernel, shape_of((groups, part, k), BF16), (), (fine_t,)), CHIPS)
    other = swap(own, "c")
    turned, rest, products, norms = call(
        own_scores_kernel,
        (shape_of((2, half_d, n), BF16), shape_of((n, half_d), BF16), shape_of((n, k), F32), shape_of((1, k), F32)),
        (), (points, own),
        cost=pl.CostEstimate(flops=8 * n * d * k, bytes_accessed=48 * n * k, transcendentals=0),
    )
    w, high, lses = call(
        functools.partial(fine_scores_kernel, scale),
        (shape_of((n, k), BF16), shape_of((1, n), F32), shape_of((far * near, 1, n), F32)),
        (), (rest, products, norms, other),
    )
    lses = exchange(lses, NEAR + ("zh",))
    send, factor = call(
        numer_send_kernel, (shape_of((half_d + 16, k), BF16), shape_of((1, n), F32)),
        (), (turned, w, high, lses),
    )
    came = swap(send, "c")
    keep = call(
        numer_keep_kernel, shape_of((half_d, k), F32), (), (turned, w, factor),
        cost=pl.CostEstimate(flops=n * d * k, bytes_accessed=6 * n * k, transcendentals=0),
    )
    tall = (part + 2) * (k // LANES)
    summed = exchange(call(pair_kernel, shape_of((groups, tall, LANES), BF16), (), (keep, came, send)), CHIPS)
    new_fine_t, blocks = call(
        new_fine_kernel, (shape_of((part, k), F32), shape_of((groups, part, k), BF16)), (), (summed, fine_t)
    )
    coarse_c, mine, core, new_fine_t = call(
        functools.partial(coarse_split_kernel, sizes),
        (shape_of((2, rows, half_d), BF16), shape_of((own_rows, d), F32), shape_of((own_rows, LANES), jnp.int32),
         shape_of((part, k), F32)),
        (), (coarse_centroids, new_fine_t),
    )
    own = exchange(blocks, CHIPS)
    other = swap(own, "c")
    products = call(
        own_coarse_kernel, shape_of((rows, k), F32), (), (coarse_c, own),
        cost=pl.CostEstimate(flops=rows * d * k, bytes_accessed=6 * rows * k, transcendentals=0),
    )
    w, high, lses = call(
        functools.partial(coarse_scores_kernel, scale),
        (shape_of((rows, k), F32), shape_of((1, k), F32), shape_of((groups * 2, 1, k), F32)),
        (), (coarse_c, products, other),
    )
    lses = exchange(lses, ("c",) + CHIPS)
    wide = d + LANES
    summed = call(
        coarse_numer_kernel, shape_of((near, near_rows * d // LANES + 16, LANES), BF16),
        (), (w, high, lses, own, other),
    )
    summed = exchange(summed, NEAR)
    summed = exchange(call(coarse_partial_kernel, shape_of((far, own_rows, wide), BF16), (), (summed,)), "zh")
    blocks = call(new_coarse_kernel, shape_of((far, own_rows, d), BF16), (), (core, summed, mine))
    blocks = call(repeat_kernel, shape_of((near, near_rows, d), BF16), (), (exchange(blocks, "zh"),))
    new_coarse = call(widen_kernel, shape_of((rows, d), F32), (), (exchange(blocks, NEAR),))
    return (new_fine_t.T, new_coarse)


def solution(mesh):
    sizes = {"y": 4, "xl": 2, "c": 2, "zh": 8, "zl": 2, "xh": 2}
    fine_mesh = Mesh(mesh.devices.reshape(tuple(sizes.values())), tuple(sizes))
    dp, mp = ("y", "xl", "c"), ("zh", "zl", "xh")
    in_specs = (P(dp, None), P(mp, dp), P(dp, None))
    out_specs = (P(mp, dp), P(dp, None))
    run = functools.partial(local, sizes)
    return jax.shard_map(run, mesh=fine_mesh, in_specs=in_specs, out_specs=out_specs, check_vma=False)
```

```python
import functools
import math

import jax
import jax.numpy as jnp
from jax import lax
from jax.experimental import pallas as pl
from jax.experimental.pallas import tpu as pltpu
from jax.sharding import Mesh, PartitionSpec as P

PRIOR = 1.0
F32, BF16 = jnp.float32, jnp.bfloat16
LANES = 128
PAIR = [(0, 1), (1, 0)]
CHIPS = ("xl", "y")
NEAR = ("xh", "zl")
CHIP_COUNT = 8
ORDER = (0, 2, 4, 6, 1, 3, 5, 7)
ORDER_BACK = (0, 4, 1, 5, 2, 6, 3, 7)
VMEM = pl.BlockSpec(memory_space=pltpu.VMEM)
SMEM = pl.BlockSpec(memory_space=pltpu.SMEM)
PARAMS = pltpu.CompilerParams(vmem_limit_bytes=24 * 1024 * 1024)


def shape_of(shape, dtype):
    return jax.ShapeDtypeStruct(shape, dtype)


def call(kernel, out_shape, scalars, arrays, scratch=(), cost=None):
    specs = [SMEM] * len(scalars) + [VMEM] * len(arrays)
    outs = jax.tree.map(lambda _: VMEM, out_shape)
    return pl.pallas_call(
        kernel, out_shape=out_shape, in_specs=specs, out_specs=outs,
        scratch_shapes=list(scratch), compiler_params=PARAMS, cost_estimate=cost,
    )(*scalars, *arrays)


def spread(block, axis, size):
    return exchange(jnp.broadcast_to(block[None], (size,) + block.shape), axis)


def exchange(blocks, axis):
    return lax.all_to_all(blocks, axis, split_axis=0, concat_axis=0, tiled=True)


def swap(block, axis):
    return lax.ppermute(block, axis, PAIR)


def to_row(column):
    return jnp.broadcast_to(column, (column.shape[0], LANES)).T[0:1, :]


def high_low(value):
    high = value.astype(BF16)
    return high, (value - high.astype(F32)).astype(BF16)


def flat(ref):
    return ref[...].reshape(ref.shape[0] * ref.shape[1], ref.shape[2])


def by_core(columns):
    part = columns.shape[0] // (2 * CHIP_COUNT)
    parts = [columns[at:at + part] for at in range(0, columns.shape[0], part)]
    return [jnp.concatenate([parts[2 * chip + core] for chip in ORDER], axis=0) for core in range(2)]


def first_kernel(fine_ref, out_ref):
    out_ref[...] = jnp.broadcast_to(fine_ref[...].astype(BF16)[None], out_ref.shape)


def coarse_split_kernel(sizes, coarse_ref, new_ref, coarse_c_ref, mine_ref, core_ref, new_fine_ref):
    core = lax.axis_index("c")
    slots = (core, 1 - core)
    own = mine_ref.shape[0]
    block = (lax.axis_index("xh") * sizes["zl"] + lax.axis_index("zl")) * sizes["zh"] + lax.axis_index("zh")
    mine_ref[...] = coarse_ref[pl.ds(pl.multiple_of(block * own, own), own), :]
    core_ref[...] = jnp.full(core_ref.shape, core, jnp.int32)
    new_fine_ref[...] = new_ref[...]
    for at, columns in enumerate(by_core(coarse_ref[...].astype(BF16).T)):
        coarse_c_ref[slots[at]] = columns.T


def own_scores_kernel(points_ref, own_ref, turned_ref, rest_ref, products_ref, norms_ref):
    core = lax.axis_index("c")
    slots = (core, 1 - core)
    own = flat(own_ref)
    norms_ref[...] = norms_of(own)
    n = products_ref.shape[0]
    tile = min(512, n)
    for start in range(0, n, tile):
        for at, columns in enumerate(by_core(points_ref[start:start + tile, :].T)):
            turned_ref[slots[at], :, start:start + tile] = columns
        rest_ref[start:start + tile, :] = turned_ref[1, :, start:start + tile].T
        products_ref[start:start + tile, :] = jnp.dot(
            turned_ref[0, :, start:start + tile].T, own, preferred_element_type=F32
        )


def norms_of(features):
    total = jnp.zeros((1, features.shape[1]), F32)
    for start in range(0, features.shape[0], LANES):
        total = total + jnp.sum(jnp.square(features[start:start + LANES].astype(F32)), axis=0, keepdims=True)
    return total


def fine_scores_kernel(scale, points_ref, products_ref, norms_ref, other_ref, w_ref, high_ref, lse_ref):
    other = flat(other_ref)
    norms = (norms_ref[...] + norms_of(other)) / scale
    n = products_ref.shape[0]
    tile = min(512, n)
    for start in range(0, n, tile):
        products = products_ref[start:start + tile, :] + jnp.dot(
            points_ref[start:start + tile, :], other, preferred_element_type=F32
        )
        scores = products * (2.0 / scale) - norms
        high = jnp.max(scores, axis=1, keepdims=True)
        weights = jnp.exp2(scores - high)
        w_ref[start:start + tile, :] = weights.astype(BF16)
        lse = to_row(high + jnp.log2(jnp.sum(weights, axis=1, keepdims=True)))
        high_ref[:, start:start + tile] = to_row(high)
        lse_ref[:, :, start:start + tile] = jnp.broadcast_to(lse[None], (lse_ref.shape[0], 1, tile))


def log_sum(ref):
    rows = ref[:, 0, :]
    top = jnp.max(rows, axis=0, keepdims=True)
    return top + jnp.log2(jnp.sum(jnp.exp2(rows - top), axis=0, keepdims=True))


def numer_send_kernel(points_t_ref, w_ref, high_ref, lses_ref, send_ref, factor_ref):
    factor = jnp.exp2(high_ref[...] - log_sum(lses_ref))
    factor_ref[...] = factor
    _, half, n = points_t_ref.shape
    scaled = (points_t_ref[1].astype(F32) * factor).astype(BF16)
    high, low = high_low(factor)
    left = jnp.concatenate([scaled, high, low, jnp.zeros((14, n), BF16)], axis=0)
    sums = jnp.dot(left, w_ref[...], preferred_element_type=F32)
    send_ref[0:half, :] = sums[0:half].astype(BF16)
    high, low = high_low(sums[half:half + 1] + sums[half + 1:half + 2])
    send_ref[half:half + 16, :] = jnp.concatenate([high, low, jnp.zeros((14, high.shape[1]), BF16)], axis=0)


def numer_keep_kernel(points_t_ref, w_ref, factor_ref, keep_ref):
    scaled = (points_t_ref[0].astype(F32) * factor_ref[...]).astype(BF16)
    keep_ref[...] = jnp.dot(scaled, w_ref[...], preferred_element_type=F32)


def pair_kernel(keep_ref, came_ref, sent_ref, out_ref):
    groups = out_ref.shape[0]
    half, k = keep_ref.shape
    part, blocks = half // groups, k // LANES
    numer = (keep_ref[...] + came_ref[0:half, :].astype(F32)).astype(BF16)
    tail = came_ref[half:half + 16, :].astype(F32) + sent_ref[half:half + 16, :].astype(F32)
    counts = tail[0:1] + tail[1:2]
    counts = jnp.concatenate([counts[:, at:at + LANES] for at in range(0, k, LANES)], axis=0)
    counts = jnp.concatenate(high_low(counts), axis=0)
    for group in range(groups):
        for block in range(blocks):
            out_ref[group, block * part:(block + 1) * part, :] = numer[
                group * part:(group + 1) * part, block * LANES:(block + 1) * LANES
            ]
        out_ref[group, blocks * part:blocks * part + 2 * blocks, :] = counts


def new_fine_kernel(came_ref, fine_ref, new_ref, send_ref):
    groups = came_ref.shape[0]
    part, k = new_ref.shape
    blocks = k // LANES
    counts = jnp.sum(came_ref[:, blocks * part:blocks * part + 2 * blocks, :].astype(F32), axis=0)
    counts = counts[0:blocks] + counts[blocks:2 * blocks] + PRIOR
    for block in range(blocks):
        lanes = slice(block * LANES, (block + 1) * LANES)
        numer = jnp.sum(came_ref[:, block * part:(block + 1) * part, :].astype(F32), axis=0)
        new = (numer + fine_ref[:, lanes]) / counts[block:block + 1]
        new_ref[:, lanes] = new
        send_ref[:, :, lanes] = jnp.broadcast_to(new.astype(BF16)[None], (groups, part, LANES))


def own_coarse_kernel(coarse_ref, own_ref, products_ref):
    products_ref[...] = jnp.dot(coarse_ref[0], flat(own_ref), preferred_element_type=F32)


def coarse_scores_kernel(scale, coarse_ref, products_ref, other_ref, w_ref, high_ref, lse_ref):
    norms = jnp.zeros((coarse_ref.shape[1], 1), F32)
    for half in range(2):
        norms = norms + jnp.sum(jnp.square(coarse_ref[half].astype(F32)), axis=1, keepdims=True)
    norms = norms / scale
    products = products_ref[...] + jnp.dot(coarse_ref[1], flat(other_ref), preferred_element_type=F32)
    scores = products * (2.0 / scale) - norms
    high = jnp.max(scores, axis=0, keepdims=True)
    weights = jnp.exp2(scores - high)
    w_ref[...] = weights
    high_ref[...] = high
    lse = high + jnp.log2(jnp.sum(weights, axis=0, keepdims=True))
    lse_ref[...] = jnp.broadcast_to(lse[None], lse_ref.shape)


def tail_of(counts):
    lane = lax.broadcasted_iota(jnp.int32, (counts.shape[0], LANES), 1)
    high = counts.astype(BF16).astype(F32)
    return jnp.where(lane == 0, high, jnp.where(lane == 1, counts - high, 0.0)).astype(BF16)


def coarse_numer_kernel(w_ref, high_ref, lses_ref, own_ref, other_ref, send_ref):
    factor = jnp.exp2(high_ref[...] - log_sum(lses_ref))
    assigned = w_ref[...] * factor
    assigned_b = assigned.astype(BF16)
    near, tall, _ = send_ref.shape
    rows = assigned.shape[0] // near
    lane_blocks = (tall - 16) // rows
    for half, ref in enumerate((own_ref, other_ref)):
        numer = lax.dot_general(
            assigned_b, flat(ref), (((1,), (1,)), ((), ())), preferred_element_type=F32
        ).astype(BF16).reshape(near, rows, lane_blocks // 2 * LANES)
        for block in range(lane_blocks // 2):
            at = (half * (lane_blocks // 2) + block) * rows
            send_ref[:, at:at + rows, :] = numer[:, :, block * LANES:(block + 1) * LANES]
    counts = to_row(jnp.sum(assigned, axis=1, keepdims=True))
    counts = jnp.concatenate([counts[:, at:at + LANES] for at in range(0, counts.shape[1], LANES)], axis=0)
    high = counts.astype(BF16).astype(F32)
    pad = jnp.zeros((16 - 2 * counts.shape[0], LANES), F32)
    tail = jnp.concatenate([high, counts - high, pad], axis=0).astype(BF16)
    send_ref[:, tall - 16:tall, :] = jnp.broadcast_to(tail[None], (near, 16, LANES))


def coarse_partial_kernel(came_ref, send_ref):
    far, own, wide = send_ref.shape
    rows, lane_blocks = far * own, wide // LANES - 1
    for block in range(lane_blocks):
        numer = jnp.sum(came_ref[:, block * rows:(block + 1) * rows, :].astype(F32), axis=0)
        send_ref[:, :, block * LANES:(block + 1) * LANES] = numer.astype(BF16).reshape(far, own, LANES)
    tail = jnp.sum(came_ref[:, lane_blocks * rows:lane_blocks * rows + 16, :].astype(F32), axis=0)
    counts = jnp.where(lax.axis_index("xh") == 0, tail[0:1] + tail[2:3], tail[1:2] + tail[3:4])
    column = jnp.broadcast_to(counts, (LANES, LANES)).T
    column = jnp.where(lax.axis_index("zl") == 0, column[0:rows], column[rows:2 * rows])
    send_ref[:, :, lane_blocks * LANES:wide] = tail_of(column[:, 0:1]).reshape(far, own, LANES)


def new_coarse_kernel(core_ref, came_ref, mine_ref, send_ref):
    d = send_ref.shape[2]
    half_d, part = d // 2, d // (2 * CHIP_COUNT)
    sums = jnp.sum(came_ref[...].astype(F32), axis=0)
    counts = sums[:, d:d + 1] + sums[:, d + 1:d + 2]
    first = core_ref[:, 0:1] == 0
    own, other = sums[:, 0:half_d], sums[:, half_d:d]
    by_core = (jnp.where(first, own, other), jnp.where(first, other, own))
    numer = jnp.concatenate(
        [by_core[core][:, at * part:(at + 1) * part] for at in ORDER_BACK for core in range(2)], axis=1
    )
    new = (numer + mine_ref[...]) / (counts + PRIOR)
    send_ref[...] = jnp.broadcast_to(new.astype(BF16)[None], send_ref.shape)


def repeat_kernel(came_ref, send_ref):
    send_ref[...] = jnp.broadcast_to(flat(came_ref)[None], send_ref.shape)


def widen_kernel(came_ref, out_ref):
    out_ref[...] = came_ref[0].astype(F32)


def widen(came):
    near, rows, d = came.shape
    return pl.pallas_call(
        widen_kernel, grid=(near,), out_shape=shape_of((near * rows, d), F32), compiler_params=PARAMS,
        in_specs=[pl.BlockSpec((1, rows, d), lambda at: (at, 0, 0))],
        out_specs=pl.BlockSpec((rows, d), lambda at: (at, 0)),
    )(came)


def local(sizes, points, fine_centroids, coarse_centroids):
    n, d = points.shape
    k, part = fine_centroids.shape
    rows = coarse_centroids.shape[0]
    groups, near, far = sizes["y"] * sizes["xl"], sizes["zl"] * sizes["xh"], sizes["zh"]
    scale = math.sqrt(d) * math.log(2.0)
    half_d, near_rows, own_rows = d // 2, rows // near, rows // (near * far)
    fine_t = fine_centroids.T

    own = exchange(call(first_kernel, shape_of((groups, part, k), BF16), (), (fine_t,)), CHIPS)
    other = swap(own, "c")
    turned, rest, products, norms = call(
        own_scores_kernel,
        (shape_of((2, half_d, n), BF16), shape_of((n, half_d), BF16), shape_of((n, k), F32), shape_of((1, k), F32)),
        (), (points, own),
        cost=pl.CostEstimate(flops=8 * n * d * k, bytes_accessed=48 * n * k, transcendentals=0),
    )
    w, high, lses = call(
        functools.partial(fine_scores_kernel, scale),
        (shape_of((n, k), BF16), shape_of((1, n), F32), shape_of((far * near, 1, n), F32)),
        (), (rest, products, norms, other),
    )
    lses = exchange(lses, NEAR + ("zh",))
    send, factor = call(
        numer_send_kernel, (shape_of((half_d + 16, k), BF16), shape_of((1, n), F32)),
        (), (turned, w, high, lses),
    )
    came = swap(send, "c")
    keep = call(
        numer_keep_kernel, shape_of((half_d, k), F32), (), (turned, w, factor),
        cost=pl.CostEstimate(flops=n * d * k, bytes_accessed=6 * n * k, transcendentals=0),
    )
    tall = (part + 2) * (k // LANES)
    summed = exchange(call(pair_kernel, shape_of((groups, tall, LANES), BF16), (), (keep, came, send)), CHIPS)
    new_fine_t, blocks = call(
        new_fine_kernel, (shape_of((part, k), F32), shape_of((groups, part, k), BF16)), (), (summed, fine_t)
    )
    coarse_c, mine, core, new_fine_t = call(
        functools.partial(coarse_split_kernel, sizes),
        (shape_of((2, rows, half_d), BF16), shape_of((own_rows, d), F32), shape_of((own_rows, LANES), jnp.int32),
         shape_of((part, k), F32)),
        (), (coarse_centroids, new_fine_t),
    )
    own = exchange(blocks, CHIPS)
    other = swap(own, "c")
    products = call(
        own_coarse_kernel, shape_of((rows, k), F32), (), (coarse_c, own),
        cost=pl.CostEstimate(flops=rows * d * k, bytes_accessed=6 * rows * k, transcendentals=0),
    )
    w, high, lses = call(
        functools.partial(coarse_scores_kernel, scale),
        (shape_of((rows, k), F32), shape_of((1, k), F32), shape_of((groups * 2, 1, k), F32)),
        (), (coarse_c, products, other),
    )
    lses = exchange(lses, ("c",) + CHIPS)
    wide = d + LANES
    summed = call(
        coarse_numer_kernel, shape_of((near, near_rows * d // LANES + 16, LANES), BF16),
        (), (w, high, lses, own, other),
    )
    summed = exchange(summed, NEAR)
    summed = exchange(call(coarse_partial_kernel, shape_of((far, own_rows, wide), BF16), (), (summed,)), "zh")
    blocks = call(new_coarse_kernel, shape_of((far, own_rows, d), BF16), (), (core, summed, mine))
    blocks = call(repeat_kernel, shape_of((near, near_rows, d), BF16), (), (exchange(blocks, "zh"),))
    new_coarse = widen(exchange(blocks, NEAR))
    return (new_fine_t.T, new_coarse)


def solution(mesh):
    sizes = {"y": 4, "xl": 2, "c": 2, "zh": 8, "zl": 2, "xh": 2}
    fine_mesh = Mesh(mesh.devices.reshape(tuple(sizes.values())), tuple(sizes))
    dp, mp = ("y", "xl", "c"), ("zh", "zl", "xh")
    in_specs = (P(dp, None), P(mp, dp), P(dp, None))
    out_specs = (P(mp, dp), P(dp, None))
    run = functools.partial(local, sizes)
    return jax.shard_map(run, mesh=fine_mesh, in_specs=in_specs, out_specs=out_specs, check_vma=False)
```

```python
import functools
import math

import jax
import jax.numpy as jnp
from jax import lax
from jax.experimental import pallas as pl
from jax.experimental.pallas import tpu as pltpu
from jax.sharding import Mesh, PartitionSpec as P

PRIOR = 1.0
F32, BF16 = jnp.float32, jnp.bfloat16
LANES = 128
PAIR = [(0, 1), (1, 0)]
CHIPS = ("xl", "y")
NEAR = ("xh", "zl")
CHIP_COUNT = 8
ORDER = (0, 2, 4, 6, 1, 3, 5, 7)
ORDER_BACK = (0, 4, 1, 5, 2, 6, 3, 7)
VMEM = pl.BlockSpec(memory_space=pltpu.VMEM)
SMEM = pl.BlockSpec(memory_space=pltpu.SMEM)
PARAMS = pltpu.CompilerParams(vmem_limit_bytes=24 * 1024 * 1024)


def shape_of(shape, dtype):
    return jax.ShapeDtypeStruct(shape, dtype)


def call(kernel, out_shape, scalars, arrays, scratch=(), cost=None):
    specs = [SMEM] * len(scalars) + [VMEM] * len(arrays)
    outs = jax.tree.map(lambda _: VMEM, out_shape)
    return pl.pallas_call(
        kernel, out_shape=out_shape, in_specs=specs, out_specs=outs,
        scratch_shapes=list(scratch), compiler_params=PARAMS, cost_estimate=cost,
    )(*scalars, *arrays)


def spread(block, axis, size):
    return exchange(jnp.broadcast_to(block[None], (size,) + block.shape), axis)


def exchange(blocks, axis):
    return lax.all_to_all(blocks, axis, split_axis=0, concat_axis=0, tiled=True)


def swap(block, axis):
    return lax.ppermute(block, axis, PAIR)


def to_row(column):
    return jnp.broadcast_to(column, (column.shape[0], LANES)).T[0:1, :]


def high_low(value):
    high = value.astype(BF16)
    return high, (value - high.astype(F32)).astype(BF16)


def flat(ref):
    return ref[...].reshape(ref.shape[0] * ref.shape[1], ref.shape[2])


def by_core(columns):
    part = columns.shape[0] // (2 * CHIP_COUNT)
    parts = [columns[at:at + part] for at in range(0, columns.shape[0], part)]
    return [jnp.concatenate([parts[2 * chip + core] for chip in ORDER], axis=0) for core in range(2)]


def first_kernel(fine_ref, out_ref):
    out_ref[...] = jnp.broadcast_to(fine_ref[...].astype(BF16)[None], out_ref.shape)


def coarse_split_kernel(sizes, coarse_ref, new_ref, coarse_c_ref, mine_ref, core_ref, new_fine_ref):
    core = lax.axis_index("c")
    slots = (core, 1 - core)
    own = mine_ref.shape[0]
    block = (lax.axis_index("xh") * sizes["zl"] + lax.axis_index("zl")) * sizes["zh"] + lax.axis_index("zh")
    mine_ref[...] = coarse_ref[pl.ds(pl.multiple_of(block * own, own), own), :]
    core_ref[...] = jnp.full(core_ref.shape, core, jnp.int32)
    new_fine_ref[...] = new_ref[...]
    for at, columns in enumerate(by_core(coarse_ref[...].astype(BF16).T)):
        coarse_c_ref[slots[at]] = columns.T


def own_scores_kernel(points_ref, own_ref, turned_ref, rest_ref, products_ref, norms_ref):
    core = lax.axis_index("c")
    slots = (core, 1 - core)
    own = flat(own_ref)
    norms_ref[...] = norms_of(own)
    n = products_ref.shape[0]
    tile = min(256, n)
    for start in range(0, n, tile):
        for at, columns in enumerate(by_core(points_ref[start:start + tile, :].T)):
            turned_ref[slots[at], :, start:start + tile] = columns
        rest_ref[start:start + tile, :] = turned_ref[1, :, start:start + tile].T
        products_ref[start:start + tile, :] = jnp.dot(
            turned_ref[0, :, start:start + tile].T, own, preferred_element_type=F32
        )


def norms_of(features):
    total = jnp.zeros((1, features.shape[1]), F32)
    for start in range(0, features.shape[0], LANES):
        total = total + jnp.sum(jnp.square(features[start:start + LANES].astype(F32)), axis=0, keepdims=True)
    return total


def fine_scores_kernel(scale, points_ref, products_ref, norms_ref, other_ref, w_ref, high_ref, lse_ref):
    other = flat(other_ref)
    norms = (norms_ref[...] + norms_of(other)) / scale
    n = products_ref.shape[0]
    tile = min(128, n)
    for start in range(0, n, tile):
        products = products_ref[start:start + tile, :] + jnp.dot(
            points_ref[start:start + tile, :], other, preferred_element_type=F32
        )
        scores = products * (2.0 / scale) - norms
        high = jnp.max(scores, axis=1, keepdims=True)
        weights = jnp.exp2(scores - high)
        w_ref[start:start + tile, :] = weights.astype(BF16)
        lse = to_row(high + jnp.log2(jnp.sum(weights, axis=1, keepdims=True)))
        high_ref[:, start:start + tile] = to_row(high)
        lse_ref[:, :, start:start + tile] = jnp.broadcast_to(lse[None], (lse_ref.shape[0], 1, tile))


def log_sum(ref):
    rows = ref[:, 0, :]
    top = jnp.max(rows, axis=0, keepdims=True)
    return top + jnp.log2(jnp.sum(jnp.exp2(rows - top), axis=0, keepdims=True))


def numer_send_kernel(points_t_ref, w_ref, high_ref, lses_ref, send_ref, factor_ref):
    factor = jnp.exp2(high_ref[...] - log_sum(lses_ref))
    factor_ref[...] = factor
    _, half, n = points_t_ref.shape
    scaled = (points_t_ref[1].astype(F32) * factor).astype(BF16)
    high, low = high_low(factor)
    left = jnp.concatenate([scaled, high, low, jnp.zeros((14, n), BF16)], axis=0)
    sums = jnp.dot(left, w_ref[...], preferred_element_type=F32)
    send_ref[0:half, :] = sums[0:half].astype(BF16)
    high, low = high_low(sums[half:half + 1] + sums[half + 1:half + 2])
    send_ref[half:half + 16, :] = jnp.concatenate([high, low, jnp.zeros((14, high.shape[1]), BF16)], axis=0)


def numer_keep_kernel(points_t_ref, w_ref, factor_ref, keep_ref):
    scaled = (points_t_ref[0].astype(F32) * factor_ref[...]).astype(BF16)
    keep_ref[...] = jnp.dot(scaled, w_ref[...], preferred_element_type=F32)


def pair_kernel(keep_ref, came_ref, sent_ref, out_ref):
    groups = out_ref.shape[0]
    half, k = keep_ref.shape
    part, blocks = half // groups, k // LANES
    numer = (keep_ref[...] + came_ref[0:half, :].astype(F32)).astype(BF16)
    tail = came_ref[half:half + 16, :].astype(F32) + sent_ref[half:half + 16, :].astype(F32)
    counts = tail[0:1] + tail[1:2]
    counts = jnp.concatenate([counts[:, at:at + LANES] for at in range(0, k, LANES)], axis=0)
    counts = jnp.concatenate(high_low(counts), axis=0)
    for group in range(groups):
        for block in range(blocks):
            out_ref[group, block * part:(block + 1) * part, :] = numer[
                group * part:(group + 1) * part, block * LANES:(block + 1) * LANES
            ]
        out_ref[group, blocks * part:blocks * part + 2 * blocks, :] = counts


def new_fine_kernel(came_ref, fine_ref, new_ref, send_ref):
    groups = came_ref.shape[0]
    part, k = new_ref.shape
    blocks = k // LANES
    counts = jnp.sum(came_ref[:, blocks * part:blocks * part + 2 * blocks, :].astype(F32), axis=0)
    counts = counts[0:blocks] + counts[blocks:2 * blocks] + PRIOR
    for block in range(blocks):
        lanes = slice(block * LANES, (block + 1) * LANES)
        numer = jnp.sum(came_ref[:, block * part:(block + 1) * part, :].astype(F32), axis=0)
        new = (numer + fine_ref[:, lanes]) / counts[block:block + 1]
        new_ref[:, lanes] = new
        send_ref[:, :, lanes] = jnp.broadcast_to(new.astype(BF16)[None], (groups, part, LANES))


def own_coarse_kernel(coarse_ref, own_ref, products_ref):
    products_ref[...] = jnp.dot(coarse_ref[0], flat(own_ref), preferred_element_type=F32)


def coarse_scores_kernel(scale, coarse_ref, products_ref, other_ref, w_ref, high_ref, lse_ref):
    norms = jnp.zeros((coarse_ref.shape[1], 1), F32)
    for half in range(2):
        norms = norms + jnp.sum(jnp.square(coarse_ref[half].astype(F32)), axis=1, keepdims=True)
    norms = norms / scale
    products = products_ref[...] + jnp.dot(coarse_ref[1], flat(other_ref), preferred_element_type=F32)
    scores = products * (2.0 / scale) - norms
    high = jnp.max(scores, axis=0, keepdims=True)
    weights = jnp.exp2(scores - high)
    w_ref[...] = weights
    high_ref[...] = high
    lse = high + jnp.log2(jnp.sum(weights, axis=0, keepdims=True))
    lse_ref[...] = jnp.broadcast_to(lse[None], lse_ref.shape)


def tail_of(counts):
    lane = lax.broadcasted_iota(jnp.int32, (counts.shape[0], LANES), 1)
    high = counts.astype(BF16).astype(F32)
    return jnp.where(lane == 0, high, jnp.where(lane == 1, counts - high, 0.0)).astype(BF16)


def coarse_numer_kernel(w_ref, high_ref, lses_ref, own_ref, other_ref, send_ref):
    factor = jnp.exp2(high_ref[...] - log_sum(lses_ref))
    assigned = w_ref[...] * factor
    assigned_b = assigned.astype(BF16)
    near, tall, _ = send_ref.shape
    rows = assigned.shape[0] // near
    lane_blocks = (tall - 16) // rows
    for half, ref in enumerate((own_ref, other_ref)):
        numer = lax.dot_general(
            assigned_b, flat(ref), (((1,), (1,)), ((), ())), preferred_element_type=F32
        ).astype(BF16).reshape(near, rows, lane_blocks // 2 * LANES)
        for block in range(lane_blocks // 2):
            at = (half * (lane_blocks // 2) + block) * rows
            send_ref[:, at:at + rows, :] = numer[:, :, block * LANES:(block + 1) * LANES]
    counts = to_row(jnp.sum(assigned, axis=1, keepdims=True))
    counts = jnp.concatenate([counts[:, at:at + LANES] for at in range(0, counts.shape[1], LANES)], axis=0)
    high = counts.astype(BF16).astype(F32)
    pad = jnp.zeros((16 - 2 * counts.shape[0], LANES), F32)
    tail = jnp.concatenate([high, counts - high, pad], axis=0).astype(BF16)
    send_ref[:, tall - 16:tall, :] = jnp.broadcast_to(tail[None], (near, 16, LANES))


def coarse_partial_kernel(came_ref, send_ref):
    far, own, wide = send_ref.shape
    rows, lane_blocks = far * own, wide // LANES - 1
    for block in range(lane_blocks):
        numer = jnp.sum(came_ref[:, block * rows:(block + 1) * rows, :].astype(F32), axis=0)
        send_ref[:, :, block * LANES:(block + 1) * LANES] = numer.astype(BF16).reshape(far, own, LANES)
    tail = jnp.sum(came_ref[:, lane_blocks * rows:lane_blocks * rows + 16, :].astype(F32), axis=0)
    counts = jnp.where(lax.axis_index("xh") == 0, tail[0:1] + tail[2:3], tail[1:2] + tail[3:4])
    column = jnp.broadcast_to(counts, (LANES, LANES)).T
    column = jnp.where(lax.axis_index("zl") == 0, column[0:rows], column[rows:2 * rows])
    send_ref[:, :, lane_blocks * LANES:wide] = tail_of(column[:, 0:1]).reshape(far, own, LANES)


def new_coarse_kernel(core_ref, came_ref, mine_ref, send_ref):
    d = send_ref.shape[2]
    half_d, part = d // 2, d // (2 * CHIP_COUNT)
    sums = jnp.sum(came_ref[...].astype(F32), axis=0)
    counts = sums[:, d:d + 1] + sums[:, d + 1:d + 2]
    first = core_ref[:, 0:1] == 0
    own, other = sums[:, 0:half_d], sums[:, half_d:d]
    by_core = (jnp.where(first, own, other), jnp.where(first, other, own))
    numer = jnp.concatenate(
        [by_core[core][:, at * part:(at + 1) * part] for at in ORDER_BACK for core in range(2)], axis=1
    )
    new = (numer + mine_ref[...]) / (counts + PRIOR)
    send_ref[...] = jnp.broadcast_to(new.astype(BF16)[None], send_ref.shape)


def repeat_kernel(came_ref, send_ref):
    send_ref[...] = jnp.broadcast_to(flat(came_ref)[None], send_ref.shape)


def widen_kernel(came_ref, out_ref):
    out_ref[...] = flat(came_ref).astype(F32)


def local(sizes, points, fine_centroids, coarse_centroids):
    n, d = points.shape
    k, part = fine_centroids.shape
    rows = coarse_centroids.shape[0]
    groups, near, far = sizes["y"] * sizes["xl"], sizes["zl"] * sizes["xh"], sizes["zh"]
    scale = math.sqrt(d) * math.log(2.0)
    half_d, near_rows, own_rows = d // 2, rows // near, rows // (near * far)
    fine_t = fine_centroids.T

    own = exchange(call(first_kernel, shape_of((groups, part, k), BF16), (), (fine_t,)), CHIPS)
    other = swap(own, "c")
    turned, rest, products, norms = call(
        own_scores_kernel,
        (shape_of((2, half_d, n), BF16), shape_of((n, half_d), BF16), shape_of((n, k), F32), shape_of((1, k), F32)),
        (), (points, own),
        cost=pl.CostEstimate(flops=8 * n * d * k, bytes_accessed=48 * n * k, transcendentals=0),
    )
    w, high, lses = call(
        functools.partial(fine_scores_kernel, scale),
        (shape_of((n, k), BF16), shape_of((1, n), F32), shape_of((far * near, 1, n), F32)),
        (), (rest, products, norms, other),
    )
    lses = exchange(lses, NEAR + ("zh",))
    send, factor = call(
        numer_send_kernel, (shape_of((half_d + 16, k), BF16), shape_of((1, n), F32)),
        (), (turned, w, high, lses),
    )
    came = swap(send, "c")
    keep = call(
        numer_keep_kernel, shape_of((half_d, k), F32), (), (turned, w, factor),
        cost=pl.CostEstimate(flops=n * d * k, bytes_accessed=6 * n * k, transcendentals=0),
    )
    tall = (part + 2) * (k // LANES)
    summed = exchange(call(pair_kernel, shape_of((groups, tall, LANES), BF16), (), (keep, came, send)), CHIPS)
    new_fine_t, blocks = call(
        new_fine_kernel, (shape_of((part, k), F32), shape_of((groups, part, k), BF16)), (), (summed, fine_t)
    )
    coarse_c, mine, core, new_fine_t = call(
        functools.partial(coarse_split_kernel, sizes),
        (shape_of((2, rows, half_d), BF16), shape_of((own_rows, d), F32), shape_of((own_rows, LANES), jnp.int32),
         shape_of((part, k), F32)),
        (), (coarse_centroids, new_fine_t),
    )
    own = exchange(blocks, CHIPS)
    other = swap(own, "c")
    products = call(
        own_coarse_kernel, shape_of((rows, k), F32), (), (coarse_c, own),
        cost=pl.CostEstimate(flops=rows * d * k, bytes_accessed=6 * rows * k, transcendentals=0),
    )
    w, high, lses = call(
        functools.partial(coarse_scores_kernel, scale),
        (shape_of((rows, k), F32), shape_of((1, k), F32), shape_of((groups * 2, 1, k), F32)),
        (), (coarse_c, products, other),
    )
    lses = exchange(lses, ("c",) + CHIPS)
    wide = d + LANES
    summed = call(
        coarse_numer_kernel, shape_of((near, near_rows * d // LANES + 16, LANES), BF16),
        (), (w, high, lses, own, other),
    )
    summed = exchange(summed, NEAR)
    summed = exchange(call(coarse_partial_kernel, shape_of((far, own_rows, wide), BF16), (), (summed,)), "zh")
    blocks = call(new_coarse_kernel, shape_of((far, own_rows, d), BF16), (), (core, summed, mine))
    blocks = call(repeat_kernel, shape_of((near, near_rows, d), BF16), (), (exchange(blocks, "zh"),))
    new_coarse = call(widen_kernel, shape_of((rows, d), F32), (), (exchange(blocks, NEAR),))
    return (new_fine_t.T, new_coarse)


def solution(mesh):
    sizes = {"y": 4, "xl": 2, "c": 2, "zh": 8, "zl": 2, "xh": 2}
    fine_mesh = Mesh(mesh.devices.reshape(tuple(sizes.values())), tuple(sizes))
    dp, mp = ("y", "xl", "c"), ("zh", "zl", "xh")
    in_specs = (P(dp, None), P(mp, dp), P(dp, None))
    out_specs = (P(mp, dp), P(dp, None))
    run = functools.partial(local, sizes)
    return jax.shard_map(run, mesh=fine_mesh, in_specs=in_specs, out_specs=out_specs, check_vma=False)
```
